512 devices in a mesh: rep: 8 (over y_lo, x), shard: 64 (over y_hi, z, core).
Axes of the slice: x: 4, y: 4 (y_hi: 2, y_lo: 2; y = y_hi * 2 + y_lo), z: 16, core: 2. Of those that a mesh axis runs over, the one named last changes fastest.
Arguments:
- hidden: bfloat16 [131072, 192], P(('rep', 'shard')), may hold values from -16 to 16
- cotangent: bfloat16 [131072, 5120], P(('rep', 'shard')), may hold values from -6 to 6
- master: float32 [192, 5120], P('shard'), may hold values from -0.078125 to 0.078125
- moment: float32 [192, 5120], P('shard'), may hold values from -6 to 6
- second: float32 [192, 5120], P('shard'), may hold values from 0.1 to 10
Outputs:
- input_grad: bfloat16 [131072, 192], P(('rep', 'shard'))
- master_new: float32 [192, 5120], P('shard')
- moment_new: float32 [192, 5120], P('shard')
- second_new: float32 [192, 5120], P('shard')
- updated_weights: bfloat16 [192, 5120], replicated
The draws below stay inside these ranges and needn't reach their ends.
All inputs are finite; a program needn't handle non-finite values.
Results may differ from the reference program's by a relative error of at most 0.0059.
Values may be sent and summed in bfloat16 or wider, within the bound.
A program may use at most 64 MiB of HBM per device.

```python
import math
import jax
import jax.numpy as jnp

D = 5120
ROWS = 192
TOKENS = 131072


def spiked(drawn, stream_key, source, target, blocks, factor):
    def block_of(axis_at):
        return (jnp.arange(drawn.shape[axis_at]) // (drawn.shape[axis_at] // blocks)).reshape((-1,) + (1,) * (drawn.ndim - 1 - axis_at))

    one_side = jax.random.permutation(stream_key, blocks)[block_of(target)]
    far = (block_of(target) + blocks // 2) % blocks
    return jnp.where((block_of(source) == one_side) | (block_of(source) == far), factor * drawn, drawn)


def block_levels(own_key, dims, shards, least, largest):
    gain = 1.0
    for axis_at, shards_of in shards:
        heights = jax.random.uniform(jax.random.fold_in(jax.random.fold_in(own_key, 6), axis_at), (shards_of,), jnp.float32, least / len(shards), largest / len(shards))
        gain = gain * jnp.repeat(jnp.exp(heights), dims[axis_at] // shards_of).reshape((-1,) + (1,) * (len(dims) - 1 - axis_at))
    return gain


def gaussian(stream_key, dims, width, bound, split=(), held_as=jnp.bfloat16):
    level = block_levels(stream_key, dims, split, -0.22, 0.18) if split else 1.0
    drawn = jax.random.normal(stream_key, dims, jnp.float32) * width * level
    return jnp.minimum(jnp.maximum(drawn, -bound), bound).astype(held_as)


def gaussian_with(key, dims, scale, limit, split, heavy, dtype=jnp.bfloat16):
    values = scale * jax.random.normal(key, dims, jnp.float32)
    if split:
        values = values * block_levels(key, dims, split, -0.22, 0.18)
    return jnp.clip(spiked(values, jax.random.fold_in(key, 3), *heavy), -limit, limit).astype(dtype)


def setup_inputs(seed: int = 0) -> dict:
    seeds = jax.random.split(jax.random.key(seed), 6)
    hidden = gaussian_with(seeds[0], (TOKENS, ROWS), 1.0, 16.0, ((0, 512),), (0, 1, 64, 4.0))
    cotangent = gaussian(seeds[1], (TOKENS, D), 1.0, 6.0, ((0, 512),))
    master = gaussian(seeds[2], (ROWS, D), D ** -0.5, 0.078125, ((0, 64),), jnp.float32)
    moment = gaussian(seeds[3], (ROWS, D), 1.0, 6.0, ((0, 64),), jnp.float32)
    second = jnp.clip(jnp.exp(math.log(10.0) - 4.6051702 * jax.random.uniform(seeds[4], (ROWS, D), jnp.float32) ** block_levels(seeds[4], (ROWS, D), ((0, 64),), -0.2, 0.2)), 0.1, 10.0)
    return {"hidden": hidden, "cotangent": cotangent, "master": master, "moment": moment, "second": second}


def adam_update(master, moment, second, gradient):
    moment_new = 0.9 * moment + 0.1 * gradient
    second_new = 0.95 * second + 0.05 * gradient * gradient
    first_fix = moment_new / (1.0 - 0.9 ** 10)
    second_fix = second_new / (1.0 - 0.95 ** 10)
    master_new = master - 0.01 * (first_fix / (jnp.sqrt(second_fix) + 1e-08) + 0.1 * master)
    return (master_new, moment_new, second_new)

def reference(hidden, cotangent, master, moment, second):
    weights = master.astype(jnp.bfloat16)
    input_grad = jnp.dot(cotangent, weights.T, preferred_element_type=jnp.float32).astype(jnp.bfloat16)
    gradient = jnp.dot(hidden.T, cotangent, preferred_element_type=jnp.float32) * (1.0 / jnp.sqrt(jnp.float32(TOKENS)))
    master_new, moment_new, second_new = adam_update(master, moment, second, gradient)
    return (input_grad, master_new, moment_new, second_new, master_new.astype(jnp.bfloat16))
```

```python
import functools
import math

import jax
import jax.numpy as jnp
import numpy as np
from jax import lax
from jax.experimental import pallas as pl
from jax.experimental.pallas import tpu as pltpu
from jax.sharding import PartitionSpec as P

MESH = pl.DeviceIdType.MESH
BF16 = jnp.bfloat16
F32 = jnp.float32

NZ = 16
ROWS = 192
D = 5120
TOK = 256
OWN = 3
BR = OWN * NZ
BC = D // 8
NJ = BC // 128
TILE = 16

NEAR = (1, 3, 2)
FAR = (2, 1, 3)


def constants():
    order = np.zeros((ROWS, ROWS), np.float32)
    for c in range(2):
        for h in range(2):
            for z in range(NZ):
                for i in range(OWN):
                    order[c * 96 + h * BR + z * OWN + i, h * 96 + z * 6 + c * OWN + i] = 1.0
    tiles = np.zeros((NZ * TILE, NJ * BR), np.float32)
    for z in range(NZ):
        for j in range(NJ):
            for i in range(OWN):
                tiles[z * TILE + OWN * j + i, j * BR + z * OWN + i] = 1.0
    weave = np.zeros((2, 96, 96), np.float32)
    for core in range(2):
        for c in range(2):
            for z in range(NZ):
                for i in range(OWN):
                    weave[core, z * 6 + c * OWN + i, (0 if c == core else BR) + z * OWN + i] = 1.0
    return tuple(m.astype(BF16) for m in (order, tiles, tiles.T.copy(), weave))


def adam_update(master, moment, second, gradient):
    moment_new = 0.9 * moment + 0.1 * gradient
    second_new = 0.95 * second + 0.05 * gradient * gradient
    first_fix = moment_new / (1.0 - 0.9**10)
    second_fix = second_new / (1.0 - 0.95**10)
    master_new = master - 0.01 * (first_fix / (jnp.sqrt(second_fix) + 1e-08) + 0.1 * master)
    return (master_new, moment_new, second_new)


def dot(a, b):
    return jnp.dot(a, b, preferred_element_type=F32)


def dot_t(a, b):
    return lax.dot_general(a, b, (((1,), (1,)), ((), ())), preferred_element_type=F32)


def send(src, dst, sems, k, device):
    return pltpu.make_async_remote_copy(
        src_ref=src,
        dst_ref=dst,
        send_sem=sems.at[0, k],
        recv_sem=sems.at[1, k],
        device_id=device,
        device_id_type=MESH,
    )


def device(x, y, z, core):
    return (lax.rem(y, 2) * 4 + x, lax.div(y, 2) * 32 + z * 2 + core)


def kernel(
    factor,
    hidden, cot, master, moment, second, order, tiles, tiles_t, weave,
    ig_out, master_out, moment_out, second_out, weights_out,
    hidden_v, cot_v, master_v, moment_v, second_v, order_v, tiles_v, tiles_tv, weave_v,
    states, grads, pair_s, pair_r, mine, one_s, one_r, two_s, two_r,
    z_s, z_r, unit, w_z, u_z, w_own, w_sib, u_own, u_sib, w_full, u_full,
    grad_rows, master_n, moment_n, second_n, ig_sum, ig_v,
    in_sem, cot_sem, out_sem, full_sem,
    pair_sem, one_sem, two_sem, z_sem, rep_sem,
    wz_sem, w1_sem, w2_sem, wp_sem, uz_sem, u1_sem, u2_sem, up_sem,
):
    rep, shard = lax.axis_index("rep"), lax.axis_index("shard")
    x, y_lo = lax.rem(rep, 4), lax.div(rep, 4)
    core, z, y_hi = lax.rem(shard, 2), lax.rem(lax.div(shard, 2), NZ), lax.div(shard, 32)
    y = y_hi * 2 + y_lo
    first = core == 0

    def at_xy(dx, dy):
        return device(lax.rem(x + dx, 4), lax.rem(y + dy, 4), z, core)

    def along_one(d):
        return at_xy(jnp.where(first, d, 0), jnp.where(first, 0, d))

    def along_two(d):
        return at_xy(jnp.where(first, 0, d), jnp.where(first, d, 0))

    def along_z(d):
        return device(x, y, lax.rem(z + d, NZ), core)

    sibling = device(x, y, z, 1 - core)

    barrier = pltpu.get_barrier_semaphore()
    for d in (1, 2, 3):
        pl.semaphore_signal(barrier, inc=1, device_id=along_one(d), device_id_type=MESH)
        pl.semaphore_signal(barrier, inc=1, device_id=along_two(d), device_id_type=MESH)
    pl.semaphore_signal(barrier, inc=1, device_id=sibling, device_id_type=MESH)
    for d in range(1, NZ):
        pl.semaphore_signal(barrier, inc=1, device_id=along_z(d), device_id_type=MESH)

    loads = [
        pltpu.make_async_copy(src, dst, in_sem.at[k])
        for k, (src, dst) in enumerate(
            (
                (order, order_v),
                (hidden, hidden_v),
                (master, master_v),
                (moment, moment_v),
                (second, second_v),
                (tiles, tiles_v),
                (tiles_t, tiles_tv),
                (weave, weave_v),
            )
        )
    ]

    def cot_load(k):
        cols = pl.ds(k * BC, BC)
        return pltpu.make_async_copy(cot.at[:, cols], cot_v.at[:, cols], cot_sem.at[k])

    loads[0].start()
    loads[1].start()
    for k in range(8):
        cot_load(k).start()
    for load in loads[2:]:
        load.start()

    loads[0].wait()
    loads[1].wait()
    hidden_t = dot_t(order_v[...], hidden_v[...]).astype(BF16)
    for k in range(8):
        cot_load(k).wait()
        grads[k] = dot(hidden_t, cot_v[:, k * BC : (k + 1) * BC])

    for load in loads[2:]:
        load.wait()
    states[...] = jnp.zeros_like(states)
    for s, ref in enumerate((master_v, moment_v, second_v)):
        for j in range(NJ):
            cols = pl.ds(pl.multiple_of(rep * BC + j * 128, 128), 128)
            states[s, OWN * j : OWN * (j + 1), :] = ref[:, cols]
    w_z[z] = states[0].astype(BF16)

    def block(a, b, of_first):
        dx, dy = jnp.where(of_first, a, b), jnp.where(of_first, b, a)
        to_x, to_y = lax.rem(x + dx, 4), lax.rem(y + dy, 4)
        return lax.rem(to_y, 2) * 4 + to_x, lax.div(to_y, 2) * BR

    def pair_copy(k):
        return send(pair_s.at[k], pair_r.at[k], pair_sem, k, sibling)

    for b in FAR + (0,):
        for a in FAR + (0,):
            col, row = block(a, b, jnp.logical_not(first))
            rows = pl.ds(pl.multiple_of((1 - core) * 96 + row, 16), BR)
            pair_s[a * 4 + b] = grads[col, rows, :].astype(BF16)

    pl.semaphore_wait(barrier, 6 + 1 + NZ - 1)

    for b in FAR + (0,):
        for a in FAR + (0,):
            pair_copy(a * 4 + b).start()

    def spread_z(ref, sems, d):
        return send(ref.at[z], ref.at[z], sems, d - 1, along_z(d))

    for d in range(1, NZ):
        spread_z(w_z, wz_sem, d).start()

    def one_copy(a, b):
        k = (a - 1) * 4 + b
        return send(one_s.at[k], one_r.at[k], one_sem, k, along_one(a))

    def two_copy(b):
        return send(two_s.at[b - 1], two_r.at[b - 1], two_sem, b - 1, along_two(b))

    for b in FAR + (0,):
        for a in FAR + (0,):
            pair_copy(a * 4 + b).wait_recv()
            col, row = block(a, b, first)
            rows = pl.ds(pl.multiple_of(core * 96 + row, 16), BR)
            term = grads[col, rows, :] + pair_r[a * 4 + b].astype(F32)
            if a == 0:
                mine[b] = term
            else:
                one_s[(a - 1) * 4 + b] = term.astype(BF16)
                one_copy(a, b).start()

    for b in FAR + (0,):
        term = mine[b]
        for a in NEAR:
            one_copy(a, b).wait_recv()
            term += one_r[(a - 1) * 4 + b].astype(F32)
        if b == 0:
            mine[0] = term
        else:
            two_s[b - 1] = term.astype(BF16)
            two_copy(b).start()

    def gather_z(ref, own, sems):
        for d in range(1, NZ):
            spread_z(ref, sems, d).wait_recv()
        pieces = dot(tiles_tv[...], ref[...].reshape(NZ * TILE, 128)).astype(BF16)
        for j in range(NJ):
            own[0, :, j * 128 : (j + 1) * 128] = pieces[j * BR : (j + 1) * BR]

    def gather_two(own, sems, b):
        return send(own.at[0], own.at[b], sems, b - 1, along_two(b))

    def gather_one(own, sems, a, b):
        return send(own.at[b], own.at[a * 4 + b], sems, (a - 1) * 4 + b, along_one(a))

    def gather_pair(own, sib, sems, k):
        return send(own.at[k], sib.at[k], sems, k, sibling)

    def place(own, sib, full, dx, dy):
        from_x, from_y = lax.rem(x + 4 - dx, 4), lax.rem(y + 4 - dy, 4)
        k_own = jnp.where(first, dx * 4 + dy, dy * 4 + dx)
        k_sib = jnp.where(first, dy * 4 + dx, dx * 4 + dy)
        both = jnp.concatenate([own[k_own], sib[k_sib]], axis=0)
        rows = pl.ds(pl.multiple_of(lax.div(from_y, 2) * 96, 16), 96)
        cols = pl.ds(pl.multiple_of((lax.rem(from_y, 2) * 4 + from_x) * BC, 128), BC)
        full[rows, cols] = dot(weave_v[core], both).astype(BF16)
        return rows, cols

    gather_z(w_z, w_own, wz_sem)
    for b in FAR:
        gather_two(w_own, w1_sem, b).start()

    term = mine[0]
    for b in NEAR:
        two_copy(b).wait_recv()
        term += two_r[b - 1].astype(F32)
    total = term.astype(BF16)
    stacked = jnp.concatenate([total[:, j * 128 : (j + 1) * 128] for j in range(NJ)], axis=0)
    z_s[...] = dot(tiles_v[...], stacked).astype(BF16).reshape(NZ, TILE, 128)

    def z_copy(d):
        return send(z_s.at[lax.rem(z + d, NZ)], z_r.at[d - 1], z_sem, d - 1, along_z(d))

    for d in (8, 7, 9, 6, 10, 5, 11, 4, 12, 3, 13, 2, 14, 1, 15):
        z_copy(d).start()

    for b in (0,) + NEAR:
        if b:
            gather_two(w_own, w1_sem, b).wait_recv()
        for a in FAR:
            gather_one(w_own, w2_sem, a, b).start()
        gather_pair(w_own, w_sib, wp_sem, b).start()

    term = z_s[z].astype(F32)
    for d in range(1, NZ):
        z_copy(d).wait_recv()
        term += z_r[d - 1].astype(F32)
    gradient = term * factor
    unit[0] = gradient
    u_z[z] = adam_update(states[0], states[1], states[2], gradient)[0].astype(BF16)
    for d in (8, 7, 9, 6, 10, 5, 11, 4, 12, 3, 13, 2, 14, 1, 15):
        spread_z(u_z, uz_sem, d).start()

    def rep_x(d):
        return send(unit.at[0], unit.at[d], rep_sem, d - 1, at_xy(d, 0))

    other_y = device(x, y + 1 - 2 * y_lo, z, core)
    rep_y = send(unit.at[pl.ds(0, 4)], unit.at[pl.ds(4, 4)], rep_sem, 3, other_y)
    for d in FAR:
        rep_x(d).start()
    for d in NEAR:
        rep_x(d).wait_recv()
    rep_y.start()

    groups = (((1, 0), (3, 0), (2, 0)), ((1, 1), (3, 1), (2, 1)), ((1, 3), (3, 3), (2, 3)), ((1, 2), (3, 2), (2, 2)))
    ready = (
        ((0, 0), (0, 1), (1, 0), (0, 3), (3, 0), (0, 2), (2, 0)),
        ((1, 1),),
        ((1, 3), (3, 1), (3, 3)),
        ((1, 2), (2, 1), (3, 2), (2, 3), (2, 2)),
    )

    def gather_rest(own, sib, full, sems_two, sems_pair, done):
        for step in range(5):
            if step < 4:
                for a, b in groups[step]:
                    gather_one(own, sems_two, a, b).wait_recv()
                    gather_pair(own, sib, sems_pair, a * 4 + b).start()
            if step > 0:
                for dx, dy in ready[step - 1]:
                    k_sib = jnp.where(first, dy * 4 + dx, dx * 4 + dy)
                    gather_pair(own, sib, sems_pair, k_sib).wait_recv()
                    done(*place(own, sib, full, dx, dy), dx * 4 + dy)

    gather_rest(w_own, w_sib, w_full, w2_sem, wp_sem, lambda rows, cols, k: None)
    ig_sum[...] = dot_t(cot_v[:, 0:BC], w_full[:, 0:BC])

    def ig_step(k, carry):
        cols = pl.ds(pl.multiple_of(k * BC, 128), BC)
        ig_sum[...] += dot_t(cot_v[:, cols], w_full[:, cols])
        return carry

    lax.fori_loop(1, 8, ig_step, 0)
    ig_v[...] = ig_sum[...].astype(BF16)
    stores = [pltpu.make_async_copy(ig_v, ig_out, out_sem.at[0])]
    stores[0].start()

    rep_y.wait_recv()
    for e in range(2):
        for d in range(4):
            source = lax.rem(y_lo + e, 2) * 4 + lax.rem(x + 4 - d, 4)
            for j in range(NJ):
                cols = pl.ds(pl.multiple_of(source * BC + j * 128, 128), 128)
                grad_rows[:, cols] = unit[e * 4 + d, OWN * j : OWN * (j + 1), :]
    new = adam_update(master_v[...], moment_v[...], second_v[...], grad_rows[...])
    master_n[...], moment_n[...], second_n[...] = new
    for k, (src, dst) in enumerate(((master_n, master_out), (moment_n, moment_out), (second_n, second_out))):
        stores.append(pltpu.make_async_copy(src, dst, out_sem.at[k + 1]))
        stores[-1].start()

    gather_z(u_z, u_own, uz_sem)
    for b in FAR:
        gather_two(u_own, u1_sem, b).start()
    for b in (0,) + NEAR:
        if b:
            gather_two(u_own, u1_sem, b).wait_recv()
        for a in FAR:
            gather_one(u_own, u2_sem, a, b).start()
        gather_pair(u_own, u_sib, up_sem, b).start()

    def store_full(rows, cols, k):
        copy = pltpu.make_async_copy(u_full.at[rows, cols], weights_out.at[rows, cols], full_sem.at[k])
        copy.start()
        stores.append(copy)

    gather_rest(u_own, u_sib, u_full, u2_sem, up_sem, store_full)

    for store in stores:
        store.wait()
    for k in range(16):
        pair_copy(k).wait_send()
        gather_pair(w_own, w_sib, wp_sem, k).wait_send()
        gather_pair(u_own, u_sib, up_sem, k).wait_send()
    for a in (1, 2, 3):
        two_copy(a).wait_send()
        rep_x(a).wait_send()
        gather_two(w_own, w1_sem, a).wait_send()
        gather_two(u_own, u1_sem, a).wait_send()
        for b in range(4):
            one_copy(a, b).wait_send()
            gather_one(w_own, w2_sem, a, b).wait_send()
            gather_one(u_own, u2_sem, a, b).wait_send()
    rep_y.wait_send()
    for d in range(1, NZ):
        z_copy(d).wait_send()
        spread_z(w_z, wz_sem, d).wait_send()
        spread_z(u_z, uz_sem, d).wait_send()


def local(hidden, cotangent, master, moment, second):
    factor = 1.0 / math.sqrt(hidden.shape[0] * lax.axis_size("rep") * lax.axis_size("shard"))
    any_space = pl.BlockSpec(memory_space=pl.ANY)
    vmem = pltpu.VMEM
    dma = pltpu.SemaphoreType.DMA
    blocks = lambda n, dtype=BF16: vmem((n, BR, BC), dtype)
    z_tiles = lambda n, dtype=BF16: vmem((n, TILE, 128), dtype)
    owned = vmem((OWN, D), F32)
    consts = constants()
    return pl.pallas_call(
        functools.partial(kernel, factor),
        out_shape=(
            jax.ShapeDtypeStruct((TOK, ROWS), BF16),
            jax.ShapeDtypeStruct((OWN, D), F32),
            jax.ShapeDtypeStruct((OWN, D), F32),
            jax.ShapeDtypeStruct((OWN, D), F32),
            jax.ShapeDtypeStruct((ROWS, D), BF16),
        ),
        in_specs=[any_space] * 9,
        out_specs=(any_space,) * 5,
        scratch_shapes=[
            vmem((TOK, ROWS), BF16), vmem((TOK, D), BF16), owned, owned, owned,
            *(vmem(m.shape, BF16) for m in consts),
            z_tiles(3, F32), vmem((8, ROWS, BC), F32), blocks(16), blocks(16), blocks(4, F32),
            blocks(12), blocks(12), blocks(3), blocks(3),
            z_tiles(NZ), z_tiles(NZ - 1), z_tiles(8, F32), z_tiles(NZ), z_tiles(NZ),
            blocks(16), blocks(16), blocks(16), blocks(16),
            vmem((ROWS, D), BF16), vmem((ROWS, D), BF16),
            owned, owned, owned, owned, vmem((TOK, ROWS), F32), vmem((TOK, ROWS), BF16),
            dma((8,)), dma((8,)), dma((4,)), dma((16,)),
            dma((2, 16)), dma((2, 12)), dma((2, 3)), dma((2, NZ - 1)), dma((2, 4)),
            dma((2, NZ - 1)), dma((2, 3)), dma((2, 12)), dma((2, 16)),
            dma((2, NZ - 1)), dma((2, 3)), dma((2, 12)), dma((2, 16)),
        ],
        compiler_params=pltpu.CompilerParams(
            collective_id=0, has_side_effects=True, vmem_limit_bytes=40 * 2**20
        ),
        name="adamw_step",
    )(hidden, cotangent, master, moment, second, *(jnp.asarray(m) for m in consts))


def solution(mesh):
    placed = (
        P(("rep", "shard"), None),
        P(("rep", "shard"), None),
        P("shard", None),
        P("shard", None),
        P("shard", None),
    )
    return jax.shard_map(
        local,
        mesh=mesh,
        in_specs=placed,
        out_specs=(
            P(("rep", "shard"), None),
            P("shard", None),
            P("shard", None),
            P("shard", None),
            P(),
        ),
        check_vma=False,
    )
```

```python
import functools
import math

import jax
import jax.numpy as jnp
import numpy as np
from jax import lax
from jax.experimental import pallas as pl
from jax.experimental.pallas import tpu as pltpu
from jax.sharding import PartitionSpec as P

MESH = pl.DeviceIdType.MESH
BF16 = jnp.bfloat16
F32 = jnp.float32

NZ = 16
ROWS = 192
D = 5120
TOK = 256
OWN = 3
BR = OWN * NZ
BC = D // 8
NJ = BC // 128
TILE = 16

NEAR = (1, 3, 2)
FAR = (2, 1, 3)
Z_ORDER = (8, 7, 9, 6, 10, 5, 11, 4, 12, 3, 13, 2, 14, 1, 15)
LAG = 4


def constants():
    order = np.zeros((ROWS, ROWS), np.float32)
    for c in range(2):
        for h in range(2):
            for z in range(NZ):
                for i in range(OWN):
                    order[c * 96 + h * BR + z * OWN + i, h * 96 + z * 6 + c * OWN + i] = 1.0
    tiles = np.zeros((NZ * TILE, NJ * BR), np.float32)
    for z in range(NZ):
        for j in range(NJ):
            for i in range(OWN):
                tiles[z * TILE + OWN * j + i, j * BR + z * OWN + i] = 1.0
    weave = np.zeros((2, 96, 96), np.float32)
    for core in range(2):
        for c in range(2):
            for z in range(NZ):
                for i in range(OWN):
                    weave[core, z * 6 + c * OWN + i, (0 if c == core else BR) + z * OWN + i] = 1.0
    return tuple(m.astype(BF16) for m in (order, tiles, tiles.T.copy(), weave))


def adam_update(master, moment, second, gradient):
    moment_new = 0.9 * moment + 0.1 * gradient
    second_new = 0.95 * second + 0.05 * gradient * gradient
    first_fix = moment_new / (1.0 - 0.9**10)
    second_fix = second_new / (1.0 - 0.95**10)
    master_new = master - 0.01 * (first_fix / (jnp.sqrt(second_fix) + 1e-08) + 0.1 * master)
    return (master_new, moment_new, second_new)


def dot(a, b):
    return jnp.dot(a, b, preferred_element_type=F32)


def dot_t(a, b):
    return lax.dot_general(a, b, (((1,), (1,)), ((), ())), preferred_element_type=F32)


def device(x, y, z, core):
    return (lax.rem(y, 2) * 4 + x, lax.div(y, 2) * 32 + z * 2 + core)


def kernel(
    factor,
    hidden, cot, master, moment, second, order, tiles, tiles_t, weave,
    ig_out, master_out, moment_out, second_out, weights_out,
    hidden_v, cot_v, master_v, moment_v, second_v, order_v, tiles_v, tiles_tv, weave_v,
    states, grads, pair_s, pair_r, mine, one_s, one_r, two_s, two_r,
    z_s, z_r, unit, w_z, u_z, w_own, w_sib, u_own, u_sib, w_full, grad_rows, ig_sum,
    in_sem, cot_sem, sent, pair_sem, one_sem, two_sem, z_sem, rep_sem, w_sem, u_sem, hello,
):
    rep, shard = lax.axis_index("rep"), lax.axis_index("shard")
    x, y_lo = lax.rem(rep, 4), lax.div(rep, 4)
    core, z, y_hi = lax.rem(shard, 2), lax.rem(lax.div(shard, 2), NZ), lax.div(shard, 32)
    y = y_hi * 2 + y_lo
    first = core == 0

    def at_xy(dx, dy):
        return device(lax.rem(x + dx, 4), lax.rem(y + dy, 4), z, core)

    def along_one(d):
        return at_xy(jnp.where(first, d, 0), jnp.where(first, 0, d))

    def along_two(d):
        return at_xy(jnp.where(first, 0, d), jnp.where(first, d, 0))

    def along_z(d):
        return device(x, y, lax.rem(z + d, NZ), core)

    sibling = device(x, y, z, 1 - core)

    def send(src, dst, family, recv, to):
        return pltpu.make_async_remote_copy(
            src_ref=src, dst_ref=dst, send_sem=sent.at[family], recv_sem=recv, device_id=to, device_id_type=MESH
        )

    def received(ref, recv):
        send(ref, ref, 0, recv, sibling).wait_recv()

    def signal(sem, to):
        pl.semaphore_signal(sem, inc=1, device_id=to, device_id_type=MESH)

    barrier = pltpu.get_barrier_semaphore()
    signal(barrier, sibling)
    for d in (2, 1, 3):
        signal(barrier, along_one(d))
        signal(barrier, along_two(d))
    for d in (2, NZ - 2, 1, NZ - 1):
        signal(barrier, along_z(d))

    loads = [
        pltpu.make_async_copy(src, dst, in_sem.at[k])
        for k, (src, dst) in enumerate(
            (
                (order, order_v),
                (hidden, hidden_v),
                (master, master_v),
                (moment, moment_v),
                (second, second_v),
                (tiles, tiles_v),
                (tiles_t, tiles_tv),
                (weave, weave_v),
            )
        )
    ]
    steps = [(dx, e) for dx in FAR + (0,) for e in (1, 0)]

    def cot_cols(dx, e):
        col = lax.rem(y_lo + e, 2) * 4 + lax.rem(x + dx, 4)
        return pl.ds(pl.multiple_of(col * BC, 128), BC)

    def cot_load(t):
        cols = cot_cols(*steps[t])
        return pltpu.make_async_copy(cot.at[:, cols], cot_v.at[:, cols], cot_sem.at[t])

    loads[0].start()
    loads[1].start()
    for t in range(8):
        cot_load(t).start()
    for load in loads[2:]:
        load.start()

    def local_term(t):
        cot_load(t).wait()
        grads[t] = dot(hidden_t, cot_v[:, cot_cols(*steps[t])])
        pair_s[t] = grads[t, pl.ds(pl.multiple_of((1 - core) * 96, 16), 96), :].astype(BF16)

    def pair_copy(t):
        return send(pair_s.at[t], pair_r.at[t], 0, pair_sem.at[t], sibling)

    def first_axis(t):
        pair_copy(t).wait_recv()
        dx, e = steps[t]
        for dy in (e, e + 2):
            row = lax.div(lax.rem(y + dy, 4), 2) * BR
            a, b = jnp.where(first, dx, dy), jnp.where(first, dy, dx)

            def term():
                own = grads[t, pl.ds(pl.multiple_of(core * 96 + row, 16), BR), :]
                return own + pair_r[t, pl.ds(pl.multiple_of(row, 16), BR), :].astype(F32)

            def keep():
                mine[b] = term()

            def pass_on():
                k = b * 3 + a - 1
                one_s[k] = term().astype(BF16)
                send(one_s.at[k], one_r.at[k], 1, one_sem.at[b], along_one(a)).start()

            if dx and dy:
                pass_on()
            elif dx == dy:
                keep()
            else:
                pl.when(a == 0)(keep)
                pl.when(a != 0)(pass_on)

    loads[0].wait()
    loads[1].wait()
    hidden_t = dot(order_v[...], hidden_v[...]).astype(BF16)
    for t in range(8):
        local_term(t)
        if t == 0:
            pl.semaphore_wait(barrier, 1 + 6 + 4)
            signal(hello.at[0], along_z(2))
            signal(hello.at[0], along_z(NZ - 2))
        pair_copy(t).start()
        if t >= LAG:
            first_axis(t - LAG)

    for load in loads[2:]:
        load.wait()
    states[...] = jnp.zeros_like(states)
    for s, ref in enumerate((master_v, moment_v, second_v)):
        for j in range(NJ):
            cols = pl.ds(pl.multiple_of(rep * BC + j * 128, 128), 128)
            states[s, OWN * j : OWN * (j + 1), :] = ref[:, cols]
    w_z[z] = states[0].astype(BF16)

    pl.semaphore_wait(hello.at[0], 2)
    signal(hello.at[1], along_z(4))
    signal(hello.at[1], along_z(NZ - 4))
    for t in range(8 - LAG, 8):
        first_axis(t)
    pl.semaphore_wait(hello.at[1], 2)

    def spread_z(ref, family, recv):
        for d in Z_ORDER:
            send(ref.at[z], ref.at[z], family, recv, along_z(d)).start()

    spread_z(w_z, 4, w_sem.at[0])

    for b in FAR + (0,):
        received(one_r.at[3 * b : 3 * b + 3], one_sem.at[b])
        term = mine[b]
        for k in range(3 * b, 3 * b + 3):
            term += one_r[k].astype(F32)
        if b == 0:
            mine[0] = term
        else:
            two_s[b - 1] = term.astype(BF16)
            send(two_s.at[b - 1], two_r.at[b - 1], 2, two_sem.at[0], along_two(b)).start()
    received(two_r, two_sem.at[0])
    term = mine[0]
    for b in NEAR:
        term += two_r[b - 1].astype(F32)

    total = term.astype(BF16)
    stacked = jnp.concatenate([total[:, j * 128 : (j + 1) * 128] for j in range(NJ)], axis=0)
    z_s[...] = dot(tiles_v[...], stacked).astype(BF16).reshape(NZ, TILE, 128)
    for d in Z_ORDER:
        send(z_s.at[lax.rem(z + d, NZ)], z_r.at[d - 1], 3, z_sem.at[0], along_z(d)).start()

    def gather_z(ref, own, sem):
        received(ref.at[0 : NZ - 1], sem.at[0])
        pieces = dot(tiles_tv[...], ref[...].reshape(NZ * TILE, 128)).astype(BF16)
        for j in range(NJ):
            own[0, :, j * 128 : (j + 1) * 128] = pieces[j * BR : (j + 1) * BR]

    def gather_two(own, family, sem):
        for b in FAR:
            send(own.at[0], own.at[4 * b], family + 1, sem.at[b], along_two(b)).start()

    def gather_one(own, family, sem, b):
        if b:
            received(own.at[4 * b], sem.at[b])
        for a in FAR:
            send(own.at[4 * b], own.at[4 * b + a], family + 2, sem.at[4 + b], along_one(a)).start()

    def gather_pair(own, sib, family, sem, b):
        received(own.at[4 * b + 1 : 4 * b + 4], sem.at[4 + b])
        four = pl.ds(4 * b, 4)
        send(own.at[four], sib.at[four], family + 3, sem.at[8 + b], sibling).start()

    def pair_there(sib, sem, b):
        received(sib.at[4 * b : 4 * b + 4], sem.at[8 + b])

    def place(own, sib, full, dx, dy):
        from_x, from_y = lax.rem(x + 4 - dx, 4), lax.rem(y + 4 - dy, 4)
        k_own = jnp.where(first, dy * 4 + dx, dx * 4 + dy)
        k_sib = jnp.where(first, dx * 4 + dy, dy * 4 + dx)
        both = jnp.concatenate([own[k_own], sib[k_sib]], axis=0)
        rows = pl.ds(pl.multiple_of(lax.div(from_y, 2) * 96, 16), 96)
        cols = pl.ds(pl.multiple_of((lax.rem(from_y, 2) * 4 + from_x) * BC, 128), BC)
        full[rows, cols] = dot(weave_v[core], both).astype(BF16)

    gather_z(w_z, w_own, w_sem)
    gather_two(w_own, 4, w_sem)
    for b in (0,) + NEAR:
        gather_one(w_own, 4, w_sem, b)

    received(z_r, z_sem.at[0])
    term = z_s[z].astype(F32)
    for k in range(NZ - 1):
        term += z_r[k].astype(F32)
    gradient = term * factor
    unit[0] = gradient
    u_z[z] = adam_update(states[0], states[1], states[2], gradient)[0].astype(BF16)
    spread_z(u_z, 8, u_sem.at[0])

    for d in FAR:
        send(unit.at[0], unit.at[d], 12, rep_sem.at[0], at_xy(d, 0)).start()
    received(unit.at[1:4], rep_sem.at[0])
    other_y = device(x, y + 1 - 2 * y_lo, z, core)
    rep_y = send(unit.at[pl.ds(0, 4)], unit.at[pl.ds(4, 4)], 13, rep_sem.at[1], other_y)
    rep_y.start()

    for b in (0,) + NEAR:
        gather_pair(w_own, w_sib, 4, w_sem, b)

    rep_y.wait_recv()
    for e in range(2):
        for d in range(4):
            source = lax.rem(y_lo + e, 2) * 4 + lax.rem(x + 4 - d, 4)
            for j in range(NJ):
                cols = pl.ds(pl.multiple_of(source * BC + j * 128, 128), 128)
                grad_rows[:, cols] = unit[e * 4 + d, OWN * j : OWN * (j + 1), :]
    new = adam_update(master_v[...], moment_v[...], second_v[...], grad_rows[...])
    master_out[...], moment_out[...], second_out[...] = new

    gather_z(u_z, u_own, u_sem)
    gather_two(u_own, 8, u_sem)
    gather_one(u_own, 8, u_sem, 0)
    for b in range(4):
        pair_there(w_sib, w_sem, b)
    for dx in range(4):
        for dy in range(4):
            place(w_own, w_sib, w_full, dx, dy)
    for b in NEAR:
        gather_one(u_own, 8, u_sem, b)

    ig_sum[...] = dot_t(w_full[:, 0:BC], cot_v[:, 0:BC])

    def ig_step(k, carry):
        cols = pl.ds(pl.multiple_of(k * BC, 128), BC)
        ig_sum[...] += dot_t(w_full[:, cols], cot_v[:, cols])
        return carry

    lax.fori_loop(1, 8, ig_step, 0)
    ig_out[...] = ig_sum[...].astype(BF16)

    ready = (
        ((0, 0),),
        ((0, 1), (1, 0), (1, 1)),
        ((0, 3), (3, 0), (1, 3), (3, 1), (3, 3)),
        ((0, 2), (2, 0), (1, 2), (2, 1), (3, 2), (2, 3), (2, 2)),
    )
    bs = (0,) + NEAR
    for k in range(5):
        if k < 4:
            gather_pair(u_own, u_sib, 8, u_sem, bs[k])
        if k > 0:
            pair_there(u_sib, u_sem, bs[k - 1])
            for dx, dy in ready[k - 1]:
                place(u_own, u_sib, weights_out, dx, dy)

    tiles_of = lambda ref: ref.at[0 : NZ - 1]
    for family, ref in (
        (0, pair_s), (1, one_s), (2, two_s), (3, z_r),
        (4, tiles_of(w_z)), (5, w_own.at[0:3]), (6, w_own.at[0:12]), (7, w_own),
        (8, tiles_of(u_z)), (9, u_own.at[0:3]), (10, u_own.at[0:12]), (11, u_own),
        (12, unit.at[1:4]), (13, unit.at[0:4]),
    ):
        send(ref, ref, family, pair_sem.at[0], sibling).wait_send()


def write_out(*refs):
    n = len(refs) // 2
    sems = refs[-1]
    copies = [pltpu.make_async_copy(refs[k], refs[n + k], sems.at[k]) for k in range(n)]
    for copy in copies:
        copy.start()
    for copy in copies:
        copy.wait()


def local(hidden, cotangent, master, moment, second):
    factor = 1.0 / math.sqrt(hidden.shape[0] * lax.axis_size("rep") * lax.axis_size("shard"))
    any_space = pl.BlockSpec(memory_space=pl.ANY)
    vmem = pltpu.VMEM
    dma = pltpu.SemaphoreType.DMA
    blocks = lambda n, dtype=BF16: vmem((n, BR, BC), dtype)
    z_tiles = lambda n, dtype=BF16: vmem((n, TILE, 128), dtype)
    owned = vmem((OWN, D), F32)
    pairs = vmem((8, 2 * BR, BC), BF16)
    in_hbm = lambda a: pltpu.with_memory_space_constraint(a, pltpu.HBM)
    consts = constants()
    results = pl.pallas_call(
        functools.partial(kernel, factor),
        out_shape=(vmem((ROWS, TOK), BF16), owned, owned, owned, vmem((ROWS, D), BF16)),
        in_specs=[pl.BlockSpec(memory_space=pltpu.HBM)] * 9,
        out_specs=(pl.BlockSpec(memory_space=vmem),) * 5,
        scratch_shapes=[
            vmem((ROWS, TOK), BF16), vmem((TOK, D), BF16), owned, owned, owned,
            *(vmem(m.shape, BF16) for m in consts),
            z_tiles(3, F32), vmem((8, ROWS, BC), F32), pairs, pairs, blocks(4, F32),
            blocks(12), blocks(12), blocks(3), blocks(3),
            z_tiles(NZ), z_tiles(NZ - 1), z_tiles(8, F32), z_tiles(NZ), z_tiles(NZ),
            blocks(16), blocks(16), blocks(16), blocks(16),
            vmem((ROWS, D), BF16), owned, vmem((ROWS, TOK), F32),
            dma((8,)), dma((8,)), dma((14,)), dma((8,)), dma((4,)), dma((1,)), dma((1,)), dma((2,)),
            dma((12,)), dma((12,)), pltpu.SemaphoreType.REGULAR((2,)),
        ],
        compiler_params=pltpu.CompilerParams(
            collective_id=0, has_side_effects=True, vmem_limit_bytes=40 * 2**20
        ),
        name="adamw_step",
    )(*(in_hbm(a) for a in (hidden.T, cotangent, master, moment, second, *map(jnp.asarray, consts))))
    input_grad_t, *rest = pl.pallas_call(
        write_out,
        out_shape=tuple(pltpu.HBM(r.shape, r.dtype) for r in results),
        in_specs=[pl.BlockSpec(memory_space=pltpu.VMEM)] * 5,
        out_specs=(pl.BlockSpec(memory_space=pltpu.HBM),) * 5,
        scratch_shapes=[dma((5,))],
        name="write_out",
    )(*(pltpu.with_memory_space_constraint(r, pltpu.VMEM) for r in results))
    return (input_grad_t.T, *rest)


def solution(mesh):
    placed = (
        P(("rep", "shard"), None),
        P(("rep", "shard"), None),
        P("shard", None),
        P("shard", None),
        P("shard", None),
    )
    return jax.shard_map(
        local,
        mesh=mesh,
        in_specs=placed,
        out_specs=(
            P(("rep", "shard"), None),
            P("shard", None),
            P("shard", None),
            P("shard", None),
            P(),
        ),
        check_vma=False,
    )
```

```python
import functools
import math

import jax
import jax.numpy as jnp
import numpy as np
from jax import lax
from jax.experimental import pallas as pl
from jax.experimental.pallas import tpu as pltpu
from jax.sharding import PartitionSpec as P

MESH = pl.DeviceIdType.MESH
BF16 = jnp.bfloat16
F32 = jnp.float32

NZ = 16
ROWS = 192
D = 5120
TOK = 256
OWN = 3
BR = OWN * NZ
BC = D // 8
NJ = BC // 128
TILE = 16

NEAR = (1, 3, 2)
FAR = (2, 1, 3)
Z_ORDER = (8, 7, 9, 6, 10, 5, 11, 4, 12, 3, 13, 2, 14, 1, 15)


def constants():
    order = np.zeros((ROWS, ROWS), np.float32)
    for c in range(2):
        for h in range(2):
            for z in range(NZ):
                for i in range(OWN):
                    order[c * 96 + h * BR + z * OWN + i, h * 96 + z * 6 + c * OWN + i] = 1.0
    tiles = np.zeros((NZ * TILE, NJ * BR), np.float32)
    for z in range(NZ):
        for j in range(NJ):
            for i in range(OWN):
                tiles[z * TILE + OWN * j + i, j * BR + z * OWN + i] = 1.0
    weave = np.zeros((2, 96, 96), np.float32)
    for core in range(2):
        for c in range(2):
            for z in range(NZ):
                for i in range(OWN):
                    weave[core, z * 6 + c * OWN + i, (0 if c == core else BR) + z * OWN + i] = 1.0
    return tuple(m.astype(BF16) for m in (order, tiles, tiles.T.copy(), weave))


def adam_update(master, moment, second, gradient):
    moment_new = 0.9 * moment + 0.1 * gradient
    second_new = 0.95 * second + 0.05 * gradient * gradient
    first_fix = moment_new / (1.0 - 0.9**10)
    second_fix = second_new / (1.0 - 0.95**10)
    master_new = master - 0.01 * (first_fix / (jnp.sqrt(second_fix) + 1e-08) + 0.1 * master)
    return (master_new, moment_new, second_new)


def dot(a, b):
    return jnp.dot(a, b, preferred_element_type=F32)


def dot_t(a, b):
    return lax.dot_general(a, b, (((1,), (1,)), ((), ())), preferred_element_type=F32)


def device(x, y, z, core):
    return (lax.rem(y, 2) * 4 + x, lax.div(y, 2) * 32 + z * 2 + core)


def kernel(
    factor,
    hidden, cot, master, moment, second, order, tiles, tiles_t, weave,
    ig_out, master_out, moment_out, second_out, weights_out,
    hidden_v, cot_v, master_v, moment_v, second_v, order_v, tiles_v, tiles_tv, weave_v,
    states, grads, pair_s, pair_r, mine, one_s, one_r, two_s, two_r,
    z_s, z_r, unit, w_z, u_z, w_own, w_sib, u_own, u_sib, w_full, grad_rows, ig_sum,
    in_sem, cot_sem, sent, pair_sem, one_sem, two_sem, z_sem, rep_sem, w_sem, u_sem, hello,
):
    rep, shard = lax.axis_index("rep"), lax.axis_index("shard")
    x, y_lo = lax.rem(rep, 4), lax.div(rep, 4)
    core, z, y_hi = lax.rem(shard, 2), lax.rem(lax.div(shard, 2), NZ), lax.div(shard, 32)
    y = y_hi * 2 + y_lo
    first = core == 0

    def at_xy(dx, dy):
        return device(lax.rem(x + dx, 4), lax.rem(y + dy, 4), z, core)

    def along_one(d):
        return at_xy(jnp.where(first, d, 0), jnp.where(first, 0, d))

    def along_two(d):
        return at_xy(jnp.where(first, 0, d), jnp.where(first, d, 0))

    def along_z(d):
        return device(x, y, lax.rem(z + d, NZ), core)

    sibling = device(x, y, z, 1 - core)

    def send(src, dst, family, recv, to):
        return pltpu.make_async_remote_copy(
            src_ref=src, dst_ref=dst, send_sem=sent.at[family], recv_sem=recv, device_id=to, device_id_type=MESH
        )

    def received(ref, recv):
        send(ref, ref, 0, recv, sibling).wait_recv()

    def signal(sem, to):
        pl.semaphore_signal(sem, inc=1, device_id=to, device_id_type=MESH)

    barrier = pltpu.get_barrier_semaphore()
    signal(barrier, sibling)
    for d in (2, 1, 3):
        signal(barrier, along_one(d))
        signal(barrier, along_two(d))
    for d in (2, NZ - 2, 1, NZ - 1):
        signal(barrier, along_z(d))

    loads = [
        pltpu.make_async_copy(src, dst, in_sem.at[k])
        for k, (src, dst) in enumerate(
            (
                (order, order_v),
                (hidden, hidden_v),
                (master, master_v),
                (moment, moment_v),
                (second, second_v),
                (tiles, tiles_v),
                (tiles_t, tiles_tv),
                (weave, weave_v),
            )
        )
    ]
    steps = [(dx, e) for e in (0, 1) for dx in FAR + (0,)]

    def cot_cols(dx, e):
        col = lax.rem(y_lo + e, 2) * 4 + lax.rem(x + dx, 4)
        return pl.ds(pl.multiple_of(col * BC, 128), BC)

    def cot_load(t):
        cols = cot_cols(*steps[t])
        return pltpu.make_async_copy(cot.at[:, cols], cot_v.at[:, cols], cot_sem.at[t])

    loads[0].start()
    loads[1].start()
    for t in range(8):
        cot_load(t).start()
    for load in loads[2:]:
        load.start()

    def pair_copy(k):
        return send(pair_s.at[k], pair_r.at[k], 0, pair_sem.at[k], sibling)

    loads[0].wait()
    loads[1].wait()
    hidden_t = dot(order_v[...], hidden_v[...]).astype(BF16)
    for t, (dx, e) in enumerate(steps):
        k = dx * 2 + e
        cot_load(t).wait()
        grads[k] = dot(hidden_t, cot_v[:, cot_cols(dx, e)])
        pair_s[k] = grads[k, pl.ds(pl.multiple_of((1 - core) * 96, 16), 96), :].astype(BF16)
        if t == 0:
            pl.semaphore_wait(barrier, 1 + 6 + 4)
            signal(hello.at[0], along_z(2))
            signal(hello.at[0], along_z(NZ - 2))
        pair_copy(k).start()

    def first_axis(a, b):
        dx, dy = jnp.where(first, a, b), jnp.where(first, b, a)
        k = dx * 2 + lax.rem(dy, 2)
        new_0, new_1 = b in (2, 1), a in (2, 1)
        if new_0 and new_1:
            pair_copy(k).wait_recv()
        elif new_0 or new_1:
            pl.when(first if new_0 else jnp.logical_not(first))(lambda: pair_copy(k).wait_recv())
        row = pl.multiple_of(lax.div(lax.rem(y + dy, 4), 2) * BR, 16)
        term = grads[k, pl.ds(pl.multiple_of(core * 96 + row, 16), BR), :] + pair_r[k, pl.ds(row, BR), :].astype(F32)
        if a == 0:
            mine[b] = term
        else:
            n = b * 3 + a - 1
            one_s[n] = term.astype(BF16)
            send(one_s.at[n], one_r.at[n], 1, one_sem.at[b], along_one(a)).start()

    for b in FAR + (0,):
        for a in FAR + (0,):
            first_axis(a, b)
        if b == 1:
            pl.semaphore_wait(hello.at[0], 2)
            signal(hello.at[1], along_z(4))
            signal(hello.at[1], along_z(NZ - 4))

    for load in loads[2:]:
        load.wait()
    states[...] = jnp.zeros_like(states)
    for s, ref in enumerate((master_v, moment_v, second_v)):
        for j in range(NJ):
            cols = pl.ds(pl.multiple_of(rep * BC + j * 128, 128), 128)
            states[s, OWN * j : OWN * (j + 1), :] = ref[:, cols]
    w_z[z] = states[0].astype(BF16)

    pl.semaphore_wait(hello.at[1], 2)

    def spread_z(ref, family, recv):
        for d in Z_ORDER:
            send(ref.at[z], ref.at[z], family, recv, along_z(d)).start()

    spread_z(w_z, 4, w_sem.at[0])

    for b in FAR + (0,):
        received(one_r.at[3 * b : 3 * b + 3], one_sem.at[b])
        term = mine[b]
        for k in range(3 * b, 3 * b + 3):
            term += one_r[k].astype(F32)
        if b == 0:
            mine[0] = term
        else:
            two_s[b - 1] = term.astype(BF16)
            send(two_s.at[b - 1], two_r.at[b - 1], 2, two_sem.at[0], along_two(b)).start()
    received(two_r, two_sem.at[0])
    term = mine[0]
    for b in NEAR:
        term += two_r[b - 1].astype(F32)

    total = term.astype(BF16)
    stacked = jnp.concatenate([total[:, j * 128 : (j + 1) * 128] for j in range(NJ)], axis=0)
    z_s[...] = dot(tiles_v[...], stacked).astype(BF16).reshape(NZ, TILE, 128)
    for d in Z_ORDER:
        send(z_s.at[lax.rem(z + d, NZ)], z_r.at[d - 1], 3, z_sem.at[0], along_z(d)).start()

    def gather_z(ref, own, sem):
        received(ref.at[0 : NZ - 1], sem.at[0])
        pieces = dot(tiles_tv[...], ref[...].reshape(NZ * TILE, 128)).astype(BF16)
        for j in range(NJ):
            own[0, :, j * 128 : (j + 1) * 128] = pieces[j * BR : (j + 1) * BR]

    def gather_two(own, family, sem):
        for b in FAR:
            send(own.at[0], own.at[4 * b], family + 1, sem.at[b], along_two(b)).start()

    def gather_one(own, family, sem, b):
        if b:
            received(own.at[4 * b], sem.at[b])
        for a in FAR:
            send(own.at[4 * b], own.at[4 * b + a], family + 2, sem.at[4 + b], along_one(a)).start()

    def gather_pair(own, sib, family, sem, b):
        received(own.at[4 * b + 1 : 4 * b + 4], sem.at[4 + b])
        four = pl.ds(4 * b, 4)
        send(own.at[four], sib.at[four], family + 3, sem.at[8 + b], sibling).start()

    def pair_there(sib, sem, b):
        received(sib.at[4 * b : 4 * b + 4], sem.at[8 + b])

    def place(own, sib, full, dx, dy):
        from_x, from_y = lax.rem(x + 4 - dx, 4), lax.rem(y + 4 - dy, 4)
        k_own = jnp.where(first, dy * 4 + dx, dx * 4 + dy)
        k_sib = jnp.where(first, dx * 4 + dy, dy * 4 + dx)
        both = jnp.concatenate([own[k_own], sib[k_sib]], axis=0)
        rows = pl.ds(pl.multiple_of(lax.div(from_y, 2) * 96, 16), 96)
        cols = pl.ds(pl.multiple_of((lax.rem(from_y, 2) * 4 + from_x) * BC, 128), BC)
        full[rows, cols] = dot(weave_v[core], both).astype(BF16)

    gather_z(w_z, w_own, w_sem)
    gather_two(w_own, 4, w_sem)
    for b in (0,) + NEAR:
        gather_one(w_own, 4, w_sem, b)

    received(z_r, z_sem.at[0])
    term = z_s[z].astype(F32)
    for k in range(NZ - 1):
        term += z_r[k].astype(F32)
    gradient = term * factor
    unit[0] = gradient
    u_z[z] = adam_update(states[0], states[1], states[2], gradient)[0].astype(BF16)
    spread_z(u_z, 8, u_sem.at[0])

    for d in FAR:
        send(unit.at[0], unit.at[d], 12, rep_sem.at[0], at_xy(d, 0)).start()
    received(unit.at[1:4], rep_sem.at[0])
    other_y = device(x, y + 1 - 2 * y_lo, z, core)
    rep_y = send(unit.at[pl.ds(0, 4)], unit.at[pl.ds(4, 4)], 13, rep_sem.at[1], other_y)
    rep_y.start()

    rep_y.wait_recv()
    for e in range(2):
        for d in range(4):
            source = lax.rem(y_lo + e, 2) * 4 + lax.rem(x + 4 - d, 4)
            for j in range(NJ):
                cols = pl.ds(pl.multiple_of(source * BC + j * 128, 128), 128)
                grad_rows[:, cols] = unit[e * 4 + d, OWN * j : OWN * (j + 1), :]
    new = adam_update(master_v[...], moment_v[...], second_v[...], grad_rows[...])
    master_out[...], moment_out[...], second_out[...] = new

    for b in (0,) + NEAR:
        gather_pair(w_own, w_sib, 4, w_sem, b)

    gather_z(u_z, u_own, u_sem)
    gather_two(u_own, 8, u_sem)
    gather_one(u_own, 8, u_sem, 0)
    for b in range(4):
        pair_there(w_sib, w_sem, b)
    for dx in range(4):
        for dy in range(4):
            place(w_own, w_sib, w_full, dx, dy)
    for b in NEAR:
        gather_one(u_own, 8, u_sem, b)

    ig_sum[...] = dot_t(w_full[:, 0:BC], cot_v[:, 0:BC])

    def ig_step(k, carry):
        cols = pl.ds(pl.multiple_of(k * BC, 128), BC)
        ig_sum[...] += dot_t(w_full[:, cols], cot_v[:, cols])
        return carry

    lax.fori_loop(1, 8, ig_step, 0)
    ig_out[...] = ig_sum[...].astype(BF16)

    ready = (
        ((0, 0),),
        ((0, 1), (1, 0), (1, 1)),
        ((0, 3), (3, 0), (1, 3), (3, 1), (3, 3)),
        ((0, 2), (2, 0), (1, 2), (2, 1), (3, 2), (2, 3), (2, 2)),
    )
    bs = (0,) + NEAR
    for k in range(5):
        if k < 4:
            gather_pair(u_own, u_sib, 8, u_sem, bs[k])
        if k > 0:
            pair_there(u_sib, u_sem, bs[k - 1])
            for dx, dy in ready[k - 1]:
                place(u_own, u_sib, weights_out, dx, dy)

    tiles_of = lambda ref: ref.at[0 : NZ - 1]
    for family, ref in (
        (0, pair_s), (1, one_s), (2, two_s), (3, z_r),
        (4, tiles_of(w_z)), (5, w_own.at[0:3]), (6, w_own.at[0:12]), (7, w_own),
        (8, tiles_of(u_z)), (9, u_own.at[0:3]), (10, u_own.at[0:12]), (11, u_own),
        (12, unit.at[1:4]), (13, unit.at[0:4]),
    ):
        send(ref, ref, family, pair_sem.at[0], sibling).wait_send()


def write_out(*refs):
    n = len(refs) // 2
    sems = refs[-1]
    copies = [pltpu.make_async_copy(refs[k], refs[n + k], sems.at[k]) for k in range(n)]
    for copy in copies:
        copy.start()
    for copy in copies:
        copy.wait()


def local(hidden, cotangent, master, moment, second):
    factor = 1.0 / math.sqrt(hidden.shape[0] * lax.axis_size("rep") * lax.axis_size("shard"))
    any_space = pl.BlockSpec(memory_space=pl.ANY)
    vmem = pltpu.VMEM
    dma = pltpu.SemaphoreType.DMA
    blocks = lambda n, dtype=BF16: vmem((n, BR, BC), dtype)
    z_tiles = lambda n, dtype=BF16: vmem((n, TILE, 128), dtype)
    owned = vmem((OWN, D), F32)
    pairs = vmem((8, 2 * BR, BC), BF16)
    in_hbm = lambda a: pltpu.with_memory_space_constraint(a, pltpu.HBM)
    consts = constants()
    results = pl.pallas_call(
        functools.partial(kernel, factor),
        out_shape=(vmem((ROWS, TOK), BF16), owned, owned, owned, vmem((ROWS, D), BF16)),
        in_specs=[pl.BlockSpec(memory_space=pltpu.HBM)] * 9,
        out_specs=(pl.BlockSpec(memory_space=vmem),) * 5,
        scratch_shapes=[
            vmem((ROWS, TOK), BF16), vmem((TOK, D), BF16), owned, owned, owned,
            *(vmem(m.shape, BF16) for m in consts),
            z_tiles(3, F32), vmem((8, ROWS, BC), F32), pairs, pairs, blocks(4, F32),
            blocks(12), blocks(12), blocks(3), blocks(3),
            z_tiles(NZ), z_tiles(NZ - 1), z_tiles(8, F32), z_tiles(NZ), z_tiles(NZ),
            blocks(16), blocks(16), blocks(16), blocks(16),
            vmem((ROWS, D), BF16), owned, vmem((ROWS, TOK), F32),
            dma((8,)), dma((8,)), dma((14,)), dma((8,)), dma((4,)), dma((1,)), dma((1,)), dma((2,)),
            dma((12,)), dma((12,)), pltpu.SemaphoreType.REGULAR((2,)),
        ],
        compiler_params=pltpu.CompilerParams(
            collective_id=0, has_side_effects=True, vmem_limit_bytes=40 * 2**20
        ),
        name="adamw_step",
    )(*(in_hbm(a) for a in (hidden.T, cotangent, master, moment, second, *map(jnp.asarray, consts))))
    input_grad_t, *rest = pl.pallas_call(
        write_out,
        out_shape=tuple(pltpu.HBM(r.shape, r.dtype) for r in results),
        in_specs=[pl.BlockSpec(memory_space=pltpu.VMEM)] * 5,
        out_specs=(pl.BlockSpec(memory_space=pltpu.HBM),) * 5,
        scratch_shapes=[dma((5,))],
        name="write_out",
    )(*(pltpu.with_memory_space_constraint(r, pltpu.VMEM) for r in results))
    return (input_grad_t.T, *rest)


def solution(mesh):
    placed = (
        P(("rep", "shard"), None),
        P(("rep", "shard"), None),
        P("shard", None),
        P("shard", None),
        P("shard", None),
    )
    return jax.shard_map(
        local,
        mesh=mesh,
        in_specs=placed,
        out_specs=(
            P(("rep", "shard"), None),
            P("shard", None),
            P("shard", None),
            P("shard", None),
            P(),
        ),
        check_vma=False,
    )
```

```python
import functools
import math

import jax
import jax.numpy as jnp
import numpy as np
from jax import lax
from jax.experimental import pallas as pl
from jax.experimental.pallas import tpu as pltpu
from jax.sharding import PartitionSpec as P

MESH = pl.DeviceIdType.MESH
BF16 = jnp.bfloat16
F32 = jnp.float32

NZ = 16
ROWS = 192
D = 5120
TOK = 256
OWN = 3
BR = OWN * NZ
BC = D // 8
NJ = BC // 128
TILE = 16

NEAR = (1, 3, 2)
FAR = (2, 1, 3)
Z_NEAR_FIRST = (0, 1, 15, 2, 14, 3, 13, 4, 12, 5, 11, 6, 10, 7, 9, 8)
CUT = 32
Z_ORDER = (8, 7, 9, 6, 10, 5, 11, 4, 12, 3, 13, 2, 14, 1, 15)


def constants():
    order = np.zeros((ROWS, ROWS), np.float32)
    for c in range(2):
        for h in range(2):
            for z in range(NZ):
                for i in range(OWN):
                    order[c * 96 + h * BR + z * OWN + i, h * 96 + z * 6 + c * OWN + i] = 1.0
    tiles = np.zeros((NZ * TILE, NJ * BR), np.float32)
    for z in range(NZ):
        for j in range(NJ):
            for i in range(OWN):
                tiles[z * TILE + OWN * j + i, j * BR + z * OWN + i] = 1.0
    slots_a, slots_b = (0, 1, 2, 3, 4, 5, 11, 12, 13, 14, 15), (6, 7, 8, 9, 10, 11)
    near = np.zeros((NJ * CUT, len(slots_a) * TILE), np.float32)
    far = np.zeros((NJ * (BR - CUT), len(slots_b) * TILE), np.float32)
    weave = np.zeros((NZ, 2, 96, 96), np.float32)
    for n, d in enumerate(Z_NEAR_FIRST):
        for i in range(OWN):
            r = n * OWN + i
            for j in range(NJ):
                if r < CUT:
                    near[j * CUT + r, slots_a.index(d) * TILE + OWN * j + i] = 1.0
                else:
                    far[j * (BR - CUT) + r - CUT, slots_b.index(d) * TILE + OWN * j + i] = 1.0
            for z in range(NZ):
                for core in range(2):
                    for c in range(2):
                        weave[z, core, (z - d) % NZ * 6 + c * OWN + i, (0 if c == core else BR) + r] = 1.0
    return tuple(m.astype(BF16) for m in (order, tiles, near, far, weave))


def adam_update(master, moment, second, gradient):
    moment_new = 0.9 * moment + 0.1 * gradient
    second_new = 0.95 * second + 0.05 * gradient * gradient
    first_fix = moment_new / (1.0 - 0.9**10)
    second_fix = second_new / (1.0 - 0.95**10)
    master_new = master - 0.01 * (first_fix / (jnp.sqrt(second_fix) + 1e-08) + 0.1 * master)
    return (master_new, moment_new, second_new)


def dot(a, b):
    return jnp.dot(a, b, preferred_element_type=F32)


def dot_t(a, b):
    return lax.dot_general(a, b, (((1,), (1,)), ((), ())), preferred_element_type=F32)


def device(x, y, z, core):
    return (lax.rem(y, 2) * 4 + x, lax.div(y, 2) * 32 + z * 2 + core)


def kernel(
    factor,
    hidden, cot, master, moment, second, order, tiles, tiles_a, tiles_b, weave,
    ig_out, master_out, moment_out, second_out, weights_out,
    hidden_v, cot_v, master_v, moment_v, second_v, order_v, tiles_v, tiles_av, tiles_bv, weave_v,
    states, grads, pair_s, pair_r, mine, one_s, one_r, two_s, two_r,
    z_s, z_r, unit, w_z, u_z, w_own_a, w_sib_a, w_own_b, w_sib_b, u_own_a, u_sib_a, u_own_b, u_sib_b, w_full, grad_rows, ig_sum,
    in_sem, cot_sem, sent, pair_sem, one_sem, two_sem, z_sem, rep_sem, w_sem, u_sem, hello,
):
    rep, shard = lax.axis_index("rep"), lax.axis_index("shard")
    x, y_lo = lax.rem(rep, 4), lax.div(rep, 4)
    core, z, y_hi = lax.rem(shard, 2), lax.rem(lax.div(shard, 2), NZ), lax.div(shard, 32)
    y = y_hi * 2 + y_lo
    first = core == 0

    def at_xy(dx, dy):
        return device(lax.rem(x + dx, 4), lax.rem(y + dy, 4), z, core)

    def along_one(d):
        return at_xy(jnp.where(first, d, 0), jnp.where(first, 0, d))

    def along_two(d):
        return at_xy(jnp.where(first, 0, d), jnp.where(first, d, 0))

    def along_z(d):
        return device(x, y, lax.rem(z + d, NZ), core)

    sibling = device(x, y, z, 1 - core)

    def send(src, dst, family, recv, to):
        return pltpu.make_async_remote_copy(
            src_ref=src, dst_ref=dst, send_sem=sent.at[family], recv_sem=recv, device_id=to, device_id_type=MESH
        )

    def received(ref, recv):
        send(ref, ref, 0, recv, sibling).wait_recv()

    def signal(sem, to):
        pl.semaphore_signal(sem, inc=1, device_id=to, device_id_type=MESH)

    loads = [
        pltpu.make_async_copy(src, dst, in_sem.at[k])
        for k, (src, dst) in enumerate(
            (
                (order, order_v),
                (hidden, hidden_v),
                (master, master_v),
                (moment, moment_v),
                (second, second_v),
                (tiles, tiles_v),
                (tiles_a, tiles_av),
                (tiles_b, tiles_bv),
                (weave.at[z, core], weave_v),
            )
        )
    ]
    steps = [(dx, e) for dx in FAR + (0,) for e in (0, 1)]

    def cot_cols(dx, e):
        col = lax.rem(y_lo + e, 2) * 4 + lax.rem(x + dx, 4)
        return pl.ds(pl.multiple_of(col * BC, 128), BC)

    def cot_load(t):
        cols = cot_cols(*steps[t])
        return pltpu.make_async_copy(cot.at[:, cols], cot_v.at[:, cols], cot_sem.at[t])

    loads[0].start()
    loads[1].start()
    for t in range(8):
        cot_load(t).start()
    barrier = pltpu.get_barrier_semaphore()
    signal(barrier, sibling)
    for d in (2, 1, 3):
        signal(barrier, along_one(d))
        signal(barrier, along_two(d))
    for d in (2, NZ - 2, 1, NZ - 1):
        signal(barrier, along_z(d))
    for load in loads[2:]:
        load.start()

    def pair_copy(k):
        return send(pair_s.at[k], pair_r.at[k], 0, pair_sem.at[k], sibling)

    loads[0].wait()
    loads[1].wait()
    hidden_t = dot(order_v[...], hidden_v[...]).astype(BF16)
    def local_term(t):
        dx, e = steps[t]
        k = dx * 2 + e
        cot_load(t).wait()
        grads[k] = dot(hidden_t, cot_v[:, cot_cols(dx, e)])
        pair_s[k] = grads[k, pl.ds(pl.multiple_of((1 - core) * 96, 16), 96), :].astype(BF16)
        if t == 0:
            pl.semaphore_wait(barrier, 1 + 6 + 4)
            signal(hello.at[0], along_z(2))
            signal(hello.at[0], along_z(NZ - 2))
        pair_copy(k).start()

    seen = (set(), set())

    def first_axis(a, b):
        dx, dy = jnp.where(first, a, b), jnp.where(first, b, a)
        k = dx * 2 + lax.rem(dy, 2)
        new = []
        for c, of_c in enumerate((a * 2 + b % 2, b * 2 + a % 2)):
            new.append(of_c not in seen[c])
            seen[c].add(of_c)
        if new[0] and new[1]:
            pair_copy(k).wait_recv()
        elif new[0] or new[1]:
            pl.when(first if new[0] else jnp.logical_not(first))(lambda: pair_copy(k).wait_recv())
        row = pl.multiple_of(lax.div(lax.rem(y + dy, 4), 2) * BR, 16)
        term = grads[k, pl.ds(pl.multiple_of(core * 96 + row, 16), BR), :] + pair_r[k, pl.ds(row, BR), :].astype(F32)
        if a == 0:
            mine[b] = term
        else:
            n = b * 3 + a - 1
            one_s[n] = term.astype(BF16)
            send(one_s.at[n], one_r.at[n], 1, one_sem.at[b], along_one(a)).start()

    for t in range(6):
        local_term(t)
    first_axis(2, 2)
    first_axis(1, 2)
    local_term(6)
    first_axis(2, 1)
    first_axis(1, 1)
    local_term(7)
    for a, b in ((3, 2), (3, 1), (2, 3), (1, 3), (3, 3), (2, 0), (1, 0), (3, 0)):
        first_axis(a, b)
    pl.semaphore_wait(hello.at[0], 2)
    signal(hello.at[1], along_z(4))
    signal(hello.at[1], along_z(NZ - 4))
    for b in FAR + (0,):
        first_axis(0, b)

    for load in loads[2:]:
        load.wait()
    states[...] = jnp.zeros_like(states)
    for s, ref in enumerate((master_v, moment_v, second_v)):
        for j in range(NJ):
            cols = pl.ds(pl.multiple_of(rep * BC + j * 128, 128), 128)
            states[s, OWN * j : OWN * (j + 1), :] = ref[:, cols]
    w_z[0] = states[0].astype(BF16)

    pl.semaphore_wait(hello.at[1], 2)

    def spread_z(ref, family, sem):
        for d in Z_ORDER:
            where = sem.at[1] if 6 <= d <= 10 else sem.at[0]
            send(ref.at[0], ref.at[d], family, where, along_z(d)).start()

    spread_z(w_z, 4, w_sem)

    for b in FAR + (0,):
        received(one_r.at[3 * b : 3 * b + 3], one_sem.at[b])
        term = mine[b]
        for k in range(3 * b, 3 * b + 3):
            term += one_r[k].astype(F32)
        if b == 0:
            mine[0] = term
        else:
            two_s[b - 1] = term.astype(BF16)
            send(two_s.at[b - 1], two_r.at[b - 1], 2, two_sem.at[0], along_two(b)).start()
    received(two_r, two_sem.at[0])
    term = mine[0]
    for b in NEAR:
        term += two_r[b - 1].astype(F32)

    total = term.astype(BF16)
    stacked = jnp.concatenate([total[:, j * 128 : (j + 1) * 128] for j in range(NJ)], axis=0)
    z_s[...] = dot(tiles_v[...], stacked).astype(BF16).reshape(NZ, TILE, 128)
    for d in Z_ORDER:
        send(z_s.at[lax.rem(z + d, NZ)], z_r.at[d - 1], 3, z_sem.at[0], along_z(d)).start()

    def gather_near(ref, own, sem):
        received(ref.at[1:11], sem.at[0])
        parts = jnp.concatenate([ref[0:6].reshape(6 * TILE, 128), ref[11:16].reshape(5 * TILE, 128)], axis=0)
        pieces = dot(tiles_av[...], parts).astype(BF16)
        for j in range(NJ):
            own[0, :, j * 128 : (j + 1) * 128] = pieces[j * CUT : (j + 1) * CUT]

    def gather_far(ref, own, sem):
        received(ref.at[6:11], sem.at[1])
        pieces = dot(tiles_bv[...], ref[6:12].reshape(6 * TILE, 128)).astype(BF16)
        rows = BR - CUT
        for j in range(NJ):
            own[0, :, j * 128 : (j + 1) * 128] = pieces[j * rows : (j + 1) * rows]

    def gather_two(part):
        own, _, family, sem, s = part
        for b in FAR:
            send(own.at[0], own.at[4 * b], family, sem.at[s + b], along_two(b)).start()

    def gather_one(part, b):
        own, _, family, sem, s = part
        if b:
            received(own.at[4 * b], sem.at[s + b])
        for a in FAR:
            send(own.at[4 * b], own.at[4 * b + a], family + 1, sem.at[s + 4 + b], along_one(a)).start()

    def gather_pair(part, b):
        own, sib, family, sem, s = part
        received(own.at[4 * b + 1 : 4 * b + 4], sem.at[s + 4 + b])
        four = pl.ds(4 * b, 4)
        send(own.at[four], sib.at[four], family + 2, sem.at[s + 8 + b], sibling).start()

    def pair_there(part, b):
        _, sib, _, sem, s = part
        received(sib.at[4 * b : 4 * b + 4], sem.at[s + 8 + b])

    w_parts = ((w_own_a, w_sib_a, 5, w_sem, 2), (w_own_b, w_sib_b, 8, w_sem, 14))
    u_parts = ((u_own_a, u_sib_a, 12, u_sem, 2), (u_own_b, u_sib_b, 15, u_sem, 14))

    def place(parts, full, dx, dy):
        from_x, from_y = lax.rem(x + 4 - dx, 4), lax.rem(y + 4 - dy, 4)
        k_own = jnp.where(first, dy * 4 + dx, dx * 4 + dy)
        k_sib = jnp.where(first, dx * 4 + dy, dy * 4 + dx)
        both = jnp.concatenate([p[0][k_own] for p in parts] + [p[1][k_sib] for p in parts], axis=0)
        rows = pl.ds(pl.multiple_of(lax.div(from_y, 2) * 96, 16), 96)
        cols = pl.ds(pl.multiple_of((lax.rem(from_y, 2) * 4 + from_x) * BC, 128), BC)
        full[rows, cols] = dot(weave_v[...], both).astype(BF16)

    gather_near(w_z, w_own_a, w_sem)
    gather_two(w_parts[0])
    gather_far(w_z, w_own_b, w_sem)
    gather_two(w_parts[1])
    for b in (0,) + NEAR:
        for part in w_parts:
            gather_one(part, b)

    received(z_r, z_sem.at[0])
    term = z_s[z].astype(F32)
    for k in range(NZ - 1):
        term += z_r[k].astype(F32)
    gradient = term * factor
    unit[0] = gradient
    u_z[0] = adam_update(states[0], states[1], states[2], gradient)[0].astype(BF16)
    spread_z(u_z, 11, u_sem)

    for d in FAR:
        send(unit.at[0], unit.at[d], 18, rep_sem.at[0], at_xy(d, 0)).start()
    received(unit.at[1:4], rep_sem.at[0])
    other_y = device(x, y + 1 - 2 * y_lo, z, core)
    rep_y = send(unit.at[pl.ds(0, 4)], unit.at[pl.ds(4, 4)], 19, rep_sem.at[1], other_y)
    rep_y.start()

    gather_near(u_z, u_own_a, u_sem)
    gather_two(u_parts[0])
    gather_one(u_parts[0], 0)
    gather_far(u_z, u_own_b, u_sem)
    gather_two(u_parts[1])
    gather_one(u_parts[1], 0)
    for b in (0,) + NEAR:
        for part in w_parts:
            gather_pair(part, b)

    rep_y.wait_recv()
    for e in range(2):
        for d in range(4):
            source = lax.rem(y_lo + e, 2) * 4 + lax.rem(x + 4 - d, 4)
            for j in range(NJ):
                cols = pl.ds(pl.multiple_of(source * BC + j * 128, 128), 128)
                grad_rows[:, cols] = unit[e * 4 + d, OWN * j : OWN * (j + 1), :]
    new = adam_update(master_v[...], moment_v[...], second_v[...], grad_rows[...])
    master_out[...], moment_out[...], second_out[...] = new

    for b in NEAR:
        for part in u_parts:
            gather_one(part, b)
    for b in range(4):
        for part in w_parts:
            pair_there(part, b)
    for dx in range(4):
        for dy in range(4):
            place(w_parts, w_full, dx, dy)

    ig_sum[...] = dot_t(w_full[:, 0:BC], cot_v[:, 0:BC])

    def ig_step(k, carry):
        cols = pl.ds(pl.multiple_of(k * BC, 128), BC)
        ig_sum[...] += dot_t(w_full[:, cols], cot_v[:, cols])
        return carry

    lax.fori_loop(1, 8, ig_step, 0)
    ig_out[...] = ig_sum[...].astype(BF16)

    ready = (
        ((0, 0),),
        ((0, 1), (1, 0), (1, 1)),
        ((0, 3), (3, 0), (1, 3), (3, 1), (3, 3)),
        ((0, 2), (2, 0), (1, 2), (2, 1), (3, 2), (2, 3), (2, 2)),
    )
    bs = (0,) + NEAR
    for k in range(5):
        if k < 4:
            for part in u_parts:
                gather_pair(part, bs[k])
        if k > 0:
            for part in u_parts:
                pair_there(part, bs[k - 1])
            for dx, dy in ready[k - 1]:
                place(u_parts, weights_out, dx, dy)

    leaving = [(0, pair_s), (1, one_s), (2, two_s), (3, z_r), (18, unit.at[1:4]), (19, unit.at[0:4])]
    for parts, ref, family in ((w_parts, w_z, 4), (u_parts, u_z, 11)):
        leaving.append((family, ref.at[0 : NZ - 1]))
        for own, _, first_family, _, _ in parts:
            leaving += [(first_family, own.at[0:3]), (first_family + 1, own.at[0:12]), (first_family + 2, own)]
    for family, ref in leaving:
        send(ref, ref, family, pair_sem.at[0], sibling).wait_send()


def write_out(*refs):
    n = len(refs) // 2
    sems = refs[-1]
    copies = [pltpu.make_async_copy(refs[k], refs[n + k], sems.at[k]) for k in range(n)]
    for copy in copies:
        copy.start()
    for copy in copies:
        copy.wait()


def local(hidden, cotangent, master, moment, second):
    factor = 1.0 / math.sqrt(hidden.shape[0] * lax.axis_size("rep") * lax.axis_size("shard"))
    any_space = pl.BlockSpec(memory_space=pl.ANY)
    vmem = pltpu.VMEM
    dma = pltpu.SemaphoreType.DMA
    blocks = lambda n, dtype=BF16: vmem((n, BR, BC), dtype)
    near, far = vmem((16, CUT, BC), BF16), vmem((16, BR - CUT, BC), BF16)
    z_tiles = lambda n, dtype=BF16: vmem((n, TILE, 128), dtype)
    owned = vmem((OWN, D), F32)
    pairs = vmem((8, 2 * BR, BC), BF16)
    in_hbm = lambda a: pltpu.with_memory_space_constraint(a, pltpu.HBM)
    consts = constants()
    results = pl.pallas_call(
        functools.partial(kernel, factor),
        out_shape=(vmem((ROWS, TOK), BF16), owned, owned, owned, vmem((ROWS, D), BF16)),
        in_specs=[pl.BlockSpec(memory_space=pltpu.HBM)] * (5 + len(consts)),
        out_specs=(pl.BlockSpec(memory_space=vmem),) * 5,
        scratch_shapes=[
            vmem((ROWS, TOK), BF16), vmem((TOK, D), BF16), owned, owned, owned,
            *(vmem(m.shape[-2:], BF16) for m in consts),
            z_tiles(3, F32), vmem((8, ROWS, BC), F32), pairs, pairs, blocks(4, F32),
            blocks(12), blocks(12), blocks(3), blocks(3),
            z_tiles(NZ), z_tiles(NZ - 1), z_tiles(8, F32), z_tiles(NZ), z_tiles(NZ),
            *((near, near, far, far) * 2),
            vmem((ROWS, D), BF16), owned, vmem((ROWS, TOK), F32),
            dma((9,)), dma((8,)), dma((20,)), dma((8,)), dma((4,)), dma((1,)), dma((1,)), dma((2,)),
            dma((26,)), dma((26,)), pltpu.SemaphoreType.REGULAR((2,)),
        ],
        compiler_params=pltpu.CompilerParams(
            collective_id=0, has_side_effects=True, vmem_limit_bytes=40 * 2**20
        ),
        name="adamw_step",
    )(*(in_hbm(a) for a in (hidden.T, cotangent, master, moment, second, *map(jnp.asarray, consts))))
    input_grad_t, *rest = pl.pallas_call(
        write_out,
        out_shape=tuple(pltpu.HBM(r.shape, r.dtype) for r in results),
        in_specs=[pl.BlockSpec(memory_space=pltpu.VMEM)] * 5,
        out_specs=(pl.BlockSpec(memory_space=pltpu.HBM),) * 5,
        scratch_shapes=[dma((5,))],
        name="write_out",
    )(*(pltpu.with_memory_space_constraint(r, pltpu.VMEM) for r in results))
    return (input_grad_t.T, *rest)


def solution(mesh):
    placed = (
        P(("rep", "shard"), None),
        P(("rep", "shard"), None),
        P("shard", None),
        P("shard", None),
        P("shard", None),
    )
    return jax.shard_map(
        local,
        mesh=mesh,
        in_specs=placed,
        out_specs=(
            P(("rep", "shard"), None),
            P("shard", None),
            P("shard", None),
            P("shard", None),
            P(),
        ),
        check_vma=False,
    )
```

```python
import functools
import math

import jax
import jax.numpy as jnp
import numpy as np
from jax import lax
from jax.experimental import pallas as pl
from jax.experimental.pallas import tpu as pltpu
from jax.sharding import PartitionSpec as P

MESH = pl.DeviceIdType.MESH
BF16 = jnp.bfloat16
F32 = jnp.float32

NZ = 16
ROWS = 192
D = 5120
TOK = 256
OWN = 3
BR = OWN * NZ
BC = D // 8
NJ = BC // 128
TILE = 16

NEAR = (1, 3, 2)
FAR = (2, 1, 3)
Z_NEAR_FIRST = (0, 1, 15, 2, 14, 3, 13, 4, 12, 5, 11, 6, 10, 7, 9, 8)
CUT = 32
Z_ORDER = (8, 7, 9, 6, 10, 5, 11, 4, 12, 3, 13, 2, 14, 1, 15)


def constants():
    order = np.zeros((ROWS, ROWS), np.float32)
    for c in range(2):
        for h in range(2):
            for z in range(NZ):
                for i in range(OWN):
                    order[c * 96 + h * BR + z * OWN + i, h * 96 + z * 6 + c * OWN + i] = 1.0
    tiles = np.zeros((NZ * TILE, NJ * BR), np.float32)
    for z in range(NZ):
        for j in range(NJ):
            for i in range(OWN):
                tiles[z * TILE + OWN * j + i, j * BR + z * OWN + i] = 1.0
    slots_a, slots_b = (0, 1, 2, 3, 4, 5, 11, 12, 13, 14, 15), (6, 7, 8, 9, 10, 11)
    near = np.zeros((NJ * CUT, len(slots_a) * TILE), np.float32)
    far = np.zeros((NJ * (BR - CUT), len(slots_b) * TILE), np.float32)
    weave = np.zeros((NZ, 2, 96, 96), np.float32)
    for n, d in enumerate(Z_NEAR_FIRST):
        for i in range(OWN):
            r = n * OWN + i
            for j in range(NJ):
                if r < CUT:
                    near[j * CUT + r, slots_a.index(d) * TILE + OWN * j + i] = 1.0
                else:
                    far[j * (BR - CUT) + r - CUT, slots_b.index(d) * TILE + OWN * j + i] = 1.0
            for z in range(NZ):
                for core in range(2):
                    for c in range(2):
                        weave[z, core, (z - d) % NZ * 6 + c * OWN + i, (0 if c == core else BR) + r] = 1.0
    return tuple(m.astype(BF16) for m in (order, tiles, near, far, weave))


def adam_update(master, moment, second, gradient):
    moment_new = 0.9 * moment + 0.1 * gradient
    second_new = 0.95 * second + 0.05 * gradient * gradient
    first_fix = moment_new / (1.0 - 0.9**10)
    second_fix = second_new / (1.0 - 0.95**10)
    master_new = master - 0.01 * (first_fix / (jnp.sqrt(second_fix) + 1e-08) + 0.1 * master)
    return (master_new, moment_new, second_new)


def dot(a, b):
    return jnp.dot(a, b, preferred_element_type=F32)


def dot_t(a, b):
    return lax.dot_general(a, b, (((1,), (1,)), ((), ())), preferred_element_type=F32)


def device(x, y, z, core):
    return (lax.rem(y, 2) * 4 + x, lax.div(y, 2) * 32 + z * 2 + core)


def kernel(
    factor,
    hidden, cot, master, moment, second, order, tiles, tiles_a, tiles_b, weave,
    ig_out, master_out, moment_out, second_out, weights_out,
    hidden_v, cot_v, master_v, moment_v, second_v, order_v, tiles_v, tiles_av, tiles_bv, weave_v,
    states, grads, pair_s, pair_r, mine, one_s, one_r, two_s, two_r,
    z_s, z_r, unit, w_z, u_z, w_own_a, w_sib_a, w_own_b, w_sib_b, u_own_a, u_sib_a, u_own_b, u_sib_b, w_full, grad_rows, ig_sum,
    in_sem, cot_sem, sent, pair_sem, one_sem, two_sem, z_sem, rep_sem, w_sem, u_sem, hello,
):
    rep, shard = lax.axis_index("rep"), lax.axis_index("shard")
    x, y_lo = lax.rem(rep, 4), lax.div(rep, 4)
    core, z, y_hi = lax.rem(shard, 2), lax.rem(lax.div(shard, 2), NZ), lax.div(shard, 32)
    y = y_hi * 2 + y_lo
    first = core == 0

    def at_xy(dx, dy):
        return device(lax.rem(x + dx, 4), lax.rem(y + dy, 4), z, core)

    def along_one(d):
        return at_xy(jnp.where(first, d, 0), jnp.where(first, 0, d))

    def along_two(d):
        return at_xy(jnp.where(first, 0, d), jnp.where(first, d, 0))

    def along_z(d):
        return device(x, y, lax.rem(z + d, NZ), core)

    sibling = device(x, y, z, 1 - core)

    def send(src, dst, family, recv, to):
        return pltpu.make_async_remote_copy(
            src_ref=src, dst_ref=dst, send_sem=sent.at[family], recv_sem=recv, device_id=to, device_id_type=MESH
        )

    def received(ref, recv):
        send(ref, ref, 0, recv, sibling).wait_recv()

    def signal(sem, to):
        pl.semaphore_signal(sem, inc=1, device_id=to, device_id_type=MESH)

    loads = [
        pltpu.make_async_copy(src, dst, in_sem.at[k])
        for k, (src, dst) in enumerate(
            (
                (order, order_v),
                (hidden, hidden_v),
                (master, master_v),
                (moment, moment_v),
                (second, second_v),
                (tiles, tiles_v),
                (tiles_a, tiles_av),
                (tiles_b, tiles_bv),
                (weave.at[z, core], weave_v),
            )
        )
    ]
    steps = [(dx, e) for dx in FAR + (0,) for e in (0, 1)]

    def cot_cols(dx, e):
        col = lax.rem(y_lo + e, 2) * 4 + lax.rem(x + dx, 4)
        return pl.ds(pl.multiple_of(col * BC, 128), BC)

    def cot_load(t):
        cols = cot_cols(*steps[t])
        return pltpu.make_async_copy(cot.at[:, cols], cot_v.at[:, cols], cot_sem.at[t])

    loads[0].start()
    loads[1].start()
    for t in range(8):
        cot_load(t).start()
    barrier = pltpu.get_barrier_semaphore()
    signal(barrier, sibling)
    for d in (2, 1, 3):
        signal(barrier, along_one(d))
        signal(barrier, along_two(d))
    for d in (2, NZ - 2, 1, NZ - 1):
        signal(barrier, along_z(d))
    for load in loads[2:]:
        load.start()

    def pair_copy(k):
        return send(pair_s.at[k], pair_r.at[k], 0, pair_sem.at[k], sibling)

    loads[0].wait()
    loads[1].wait()
    hidden_t = dot(order_v[...], hidden_v[...]).astype(BF16)
    def local_term(t):
        dx, e = steps[t]
        k = dx * 2 + e
        cot_load(t).wait()
        grads[k] = dot(hidden_t, cot_v[:, cot_cols(dx, e)])
        pair_s[k] = grads[k, pl.ds(pl.multiple_of((1 - core) * 96, 16), 96), :].astype(BF16)
        if t == 0:
            pl.semaphore_wait(barrier, 1 + 6 + 4)
            signal(hello.at[0], along_z(2))
            signal(hello.at[0], along_z(NZ - 2))
        pair_copy(k).start()

    seen = (set(), set())

    def first_axis(a, b):
        dx, dy = jnp.where(first, a, b), jnp.where(first, b, a)
        k = dx * 2 + lax.rem(dy, 2)
        new = []
        for c, of_c in enumerate((a * 2 + b % 2, b * 2 + a % 2)):
            new.append(of_c not in seen[c])
            seen[c].add(of_c)
        if new[0] and new[1]:
            pair_copy(k).wait_recv()
        elif new[0] or new[1]:
            pl.when(first if new[0] else jnp.logical_not(first))(lambda: pair_copy(k).wait_recv())
        row = pl.multiple_of(lax.div(lax.rem(y + dy, 4), 2) * BR, 16)
        term = grads[k, pl.ds(pl.multiple_of(core * 96 + row, 16), BR), :] + pair_r[k, pl.ds(row, BR), :].astype(F32)
        if a == 0:
            mine[b] = term
        else:
            n = b * 3 + a - 1
            one_s[n] = term.astype(BF16)
            send(one_s.at[n], one_r.at[n], 1, one_sem.at[b], along_one(a)).start()

    for t in range(6):
        local_term(t)
    first_axis(2, 2)
    first_axis(1, 2)
    local_term(6)
    first_axis(2, 1)
    first_axis(1, 1)
    local_term(7)
    for a, b in ((3, 2), (3, 1), (2, 3), (1, 3), (3, 3), (2, 0), (1, 0), (3, 0)):
        first_axis(a, b)
    pl.semaphore_wait(hello.at[0], 2)
    signal(hello.at[1], along_z(4))
    signal(hello.at[1], along_z(NZ - 4))
    for b in FAR + (0,):
        first_axis(0, b)

    for load in loads[2:]:
        load.wait()
    states[...] = jnp.zeros_like(states)
    for s, ref in enumerate((master_v, moment_v, second_v)):
        for j in range(NJ):
            cols = pl.ds(pl.multiple_of(rep * BC + j * 128, 128), 128)
            states[s, OWN * j : OWN * (j + 1), :] = ref[:, cols]
    w_z[0] = states[0].astype(BF16)

    pl.semaphore_wait(hello.at[1], 2)

    def spread_z(ref, family, sem):
        for d in Z_ORDER:
            where = sem.at[1] if 6 <= d <= 10 else sem.at[0]
            send(ref.at[0], ref.at[d], family, where, along_z(d)).start()

    spread_z(w_z, 4, w_sem)

    for b in FAR + (0,):
        received(one_r.at[3 * b : 3 * b + 3], one_sem.at[b])
        term = mine[b]
        for k in range(3 * b, 3 * b + 3):
            term += one_r[k].astype(F32)
        if b == 0:
            mine[0] = term
        else:
            two_s[b - 1] = term.astype(BF16)
            send(two_s.at[b - 1], two_r.at[b - 1], 2, two_sem.at[0], along_two(b)).start()
    received(two_r, two_sem.at[0])
    term = mine[0]
    for b in NEAR:
        term += two_r[b - 1].astype(F32)

    total = term.astype(BF16)
    stacked = jnp.concatenate([total[:, j * 128 : (j + 1) * 128] for j in range(NJ)], axis=0)
    z_s[...] = dot(tiles_v[...], stacked).astype(BF16).reshape(NZ, TILE, 128)
    for d in Z_ORDER:
        send(z_s.at[lax.rem(z + d, NZ)], z_r.at[d - 1], 3, z_sem.at[0], along_z(d)).start()

    def gather_near(ref, own, sem):
        received(ref.at[1:11], sem.at[0])
        parts = jnp.concatenate([ref[0:6].reshape(6 * TILE, 128), ref[11:16].reshape(5 * TILE, 128)], axis=0)
        pieces = dot(tiles_av[...], parts).astype(BF16)
        for j in range(NJ):
            own[0, :, j * 128 : (j + 1) * 128] = pieces[j * CUT : (j + 1) * CUT]

    def gather_far(ref, own, sem):
        received(ref.at[6:11], sem.at[1])
        pieces = dot(tiles_bv[...], ref[6:12].reshape(6 * TILE, 128)).astype(BF16)
        rows = BR - CUT
        for j in range(NJ):
            own[0, :, j * 128 : (j + 1) * 128] = pieces[j * rows : (j + 1) * rows]

    def gather_two(part):
        own, _, family, sem, s = part
        for b in FAR:
            send(own.at[0], own.at[4 * b], family, sem.at[s + b], along_two(b)).start()

    def gather_one(part, b):
        own, _, family, sem, s = part
        if b:
            received(own.at[4 * b], sem.at[s + b])
        for a in FAR:
            send(own.at[4 * b], own.at[4 * b + a], family + 1, sem.at[s + 4 + b], along_one(a)).start()

    def gather_pair(part, b):
        own, sib, family, sem, s = part
        received(own.at[4 * b + 1 : 4 * b + 4], sem.at[s + 4 + b])
        four = pl.ds(4 * b, 4)
        send(own.at[four], sib.at[four], family + 2, sem.at[s + 8 + b], sibling).start()

    def pair_there(part, b):
        _, sib, _, sem, s = part
        received(sib.at[4 * b : 4 * b + 4], sem.at[s + 8 + b])

    w_parts = ((w_own_a, w_sib_a, 5, w_sem, 2), (w_own_b, w_sib_b, 8, w_sem, 14))
    u_parts = ((u_own_a, u_sib_a, 12, u_sem, 2), (u_own_b, u_sib_b, 15, u_sem, 14))

    def place(parts, full, dx, dy):
        from_x, from_y = lax.rem(x + 4 - dx, 4), lax.rem(y + 4 - dy, 4)
        k_own = jnp.where(first, dy * 4 + dx, dx * 4 + dy)
        k_sib = jnp.where(first, dx * 4 + dy, dy * 4 + dx)
        both = jnp.concatenate([p[0][k_own] for p in parts] + [p[1][k_sib] for p in parts], axis=0)
        rows = pl.ds(pl.multiple_of(lax.div(from_y, 2) * 96, 16), 96)
        cols = pl.ds(pl.multiple_of((lax.rem(from_y, 2) * 4 + from_x) * BC, 128), BC)
        full[rows, cols] = dot(weave_v[...], both).astype(BF16)

    gather_near(w_z, w_own_a, w_sem)
    gather_two(w_parts[0])
    gather_far(w_z, w_own_b, w_sem)
    gather_two(w_parts[1])
    for b in (0,) + NEAR:
        for part in w_parts:
            gather_one(part, b)

    received(z_r, z_sem.at[0])
    term = z_s[z].astype(F32)
    for k in range(NZ - 1):
        term += z_r[k].astype(F32)
    gradient = term * factor
    unit[0] = gradient
    u_z[0] = adam_update(states[0], states[1], states[2], gradient)[0].astype(BF16)
    spread_z(u_z, 11, u_sem)

    for d in FAR:
        send(unit.at[0], unit.at[d], 18, rep_sem.at[0], at_xy(d, 0)).start()
    received(unit.at[1:4], rep_sem.at[0])
    other_y = device(x, y + 1 - 2 * y_lo, z, core)
    rep_y = send(unit.at[pl.ds(0, 4)], unit.at[pl.ds(4, 4)], 19, rep_sem.at[1], other_y)
    rep_y.start()

    gather_near(u_z, u_own_a, u_sem)
    gather_two(u_parts[0])
    gather_one(u_parts[0], 0)
    gather_far(u_z, u_own_b, u_sem)
    gather_two(u_parts[1])
    gather_one(u_parts[1], 0)
    for b in (0,) + NEAR:
        for part in w_parts:
            gather_pair(part, b)

    rep_y.wait_recv()
    for e in range(2):
        for d in range(4):
            source = lax.rem(y_lo + e, 2) * 4 + lax.rem(x + 4 - d, 4)
            for j in range(NJ):
                cols = pl.ds(pl.multiple_of(source * BC + j * 128, 128), 128)
                grad_rows[:, cols] = unit[e * 4 + d, OWN * j : OWN * (j + 1), :]
    new = adam_update(master_v[...], moment_v[...], second_v[...], grad_rows[...])
    master_out[...], moment_out[...], second_out[...] = new

    for part in u_parts:
        for b in NEAR:
            gather_one(part, b)
    for b in range(4):
        for part in w_parts:
            pair_there(part, b)
    for dx in range(4):
        for dy in range(4):
            place(w_parts, w_full, dx, dy)

    ig_sum[...] = dot_t(w_full[:, 0:BC], cot_v[:, 0:BC])

    def ig_step(k, carry):
        cols = pl.ds(pl.multiple_of(k * BC, 128), BC)
        ig_sum[...] += dot_t(w_full[:, cols], cot_v[:, cols])
        return carry

    lax.fori_loop(1, 8, ig_step, 0)
    ig_out[...] = ig_sum[...].astype(BF16)

    ready = (
        ((0, 0),),
        ((0, 1), (1, 0), (1, 1)),
        ((0, 3), (3, 0), (1, 3), (3, 1), (3, 3)),
        ((0, 2), (2, 0), (1, 2), (2, 1), (3, 2), (2, 3), (2, 2)),
    )
    bs = (0,) + NEAR
    for b in bs:
        gather_pair(u_parts[0], b)
    for k in range(5):
        if k < 4:
            gather_pair(u_parts[1], bs[k])
        if k > 0:
            for part in u_parts:
                pair_there(part, bs[k - 1])
            for dx, dy in ready[k - 1]:
                place(u_parts, weights_out, dx, dy)

    leaving = [(0, pair_s), (1, one_s), (2, two_s), (3, z_r), (18, unit.at[1:4]), (19, unit.at[0:4])]
    for parts, ref, family in ((w_parts, w_z, 4), (u_parts, u_z, 11)):
        leaving.append((family, ref.at[0 : NZ - 1]))
        for own, _, first_family, _, _ in parts:
            leaving += [(first_family, own.at[0:3]), (first_family + 1, own.at[0:12]), (first_family + 2, own)]
    for family, ref in leaving:
        send(ref, ref, family, pair_sem.at[0], sibling).wait_send()


def write_out(*refs):
    n = len(refs) // 2
    sems = refs[-1]
    copies = [pltpu.make_async_copy(refs[k], refs[n + k], sems.at[k]) for k in range(n)]
    for copy in copies:
        copy.start()
    for copy in copies:
        copy.wait()


def local(hidden, cotangent, master, moment, second):
    factor = 1.0 / math.sqrt(hidden.shape[0] * lax.axis_size("rep") * lax.axis_size("shard"))
    any_space = pl.BlockSpec(memory_space=pl.ANY)
    vmem = pltpu.VMEM
    dma = pltpu.SemaphoreType.DMA
    blocks = lambda n, dtype=BF16: vmem((n, BR, BC), dtype)
    near, far = vmem((16, CUT, BC), BF16), vmem((16, BR - CUT, BC), BF16)
    z_tiles = lambda n, dtype=BF16: vmem((n, TILE, 128), dtype)
    owned = vmem((OWN, D), F32)
    pairs = vmem((8, 2 * BR, BC), BF16)
    in_hbm = lambda a: pltpu.with_memory_space_constraint(a, pltpu.HBM)
    consts = constants()
    results = pl.pallas_call(
        functools.partial(kernel, factor),
        out_shape=(vmem((ROWS, TOK), BF16), owned, owned, owned, vmem((ROWS, D), BF16)),
        in_specs=[pl.BlockSpec(memory_space=pltpu.HBM)] * (5 + len(consts)),
        out_specs=(pl.BlockSpec(memory_space=vmem),) * 5,
        scratch_shapes=[
            vmem((ROWS, TOK), BF16), vmem((TOK, D), BF16), owned, owned, owned,
            *(vmem(m.shape[-2:], BF16) for m in consts),
            z_tiles(3, F32), vmem((8, ROWS, BC), F32), pairs, pairs, blocks(4, F32),
            blocks(12), blocks(12), blocks(3), blocks(3),
            z_tiles(NZ), z_tiles(NZ - 1), z_tiles(8, F32), z_tiles(NZ), z_tiles(NZ),
            *((near, near, far, far) * 2),
            vmem((ROWS, D), BF16), owned, vmem((ROWS, TOK), F32),
            dma((9,)), dma((8,)), dma((20,)), dma((8,)), dma((4,)), dma((1,)), dma((1,)), dma((2,)),
            dma((26,)), dma((26,)), pltpu.SemaphoreType.REGULAR((2,)),
        ],
        compiler_params=pltpu.CompilerParams(
            collective_id=0, has_side_effects=True, vmem_limit_bytes=40 * 2**20
        ),
        name="adamw_step",
    )(*(in_hbm(a) for a in (hidden.T, cotangent, master, moment, second, *map(jnp.asarray, consts))))
    input_grad_t, *rest = pl.pallas_call(
        write_out,
        out_shape=tuple(pltpu.HBM(r.shape, r.dtype) for r in results),
        in_specs=[pl.BlockSpec(memory_space=pltpu.VMEM)] * 5,
        out_specs=(pl.BlockSpec(memory_space=pltpu.HBM),) * 5,
        scratch_shapes=[dma((5,))],
        name="write_out",
    )(*(pltpu.with_memory_space_constraint(r, pltpu.VMEM) for r in results))
    return (input_grad_t.T, *rest)


def solution(mesh):
    placed = (
        P(("rep", "shard"), None),
        P(("rep", "shard"), None),
        P("shard", None),
        P("shard", None),
        P("shard", None),
    )
    return jax.shard_map(
        local,
        mesh=mesh,
        in_specs=placed,
        out_specs=(
            P(("rep", "shard"), None),
            P("shard", None),
            P("shard", None),
            P("shard", None),
            P(),
        ),
        check_vma=False,
    )
```
